256 devices in a mesh: row: 16 (over y, z_hi, core), col: 16 (over x, z_lo).
Axes of the slice: x: 4, y: 4, z: 8 (z_hi: 2, z_lo: 4; z = z_hi * 4 + z_lo), core: 2. Of those that a mesh axis runs over, the one named last changes fastest.
Arguments:
- inputs: bfloat16 [512, 9216], P(None, 'row'), may hold values from -6 to 6
- target: bfloat16 [512, 9216], P(None, 'row'), may hold values from -6 to 6
- w_in: bfloat16 [9216, 18432], P('row', 'col'), may hold values from -0.0625 to 0.0625
- w_out: bfloat16 [18432, 9216], P('col', 'row'), may hold values from -0.046875 to 0.046875
- probe_in: bfloat16 [9216, 18432], P('row', 'col'), may hold values from -1 to 1, as said below
- probe_out: bfloat16 [18432, 9216], P('col', 'row'), may hold values from -1 to 1, as said below
Outputs:
- hess_in: bfloat16 [9216, 18432], P('row', 'col')
- hess_out: bfloat16 [18432, 9216], P('col', 'row')
The draws below stay inside these ranges and needn't reach their ends.
Inputs may be any that keep to these rules, and one draw needn't show every extreme that they name: `probe_in`: every entry is +1 or -1. `probe_out`: every entry is +1 or -1.
All inputs are finite; a program needn't handle non-finite values.
Results may differ from the reference program's by a relative error of at most 0.0085.
Values may be sent and summed in bfloat16 or wider, within the bound.
A program may use at most 64 MiB of HBM per device.

```python
import jax
import jax.numpy as jnp
from jax import lax

D = 9216
FF = 18432
TOKENS = 512


def draw_probe_in(key, part):
    key = jax.random.fold_in(key, 11)
    flips = jax.random.bernoulli(key, 0.5, (D, FF)).astype(jnp.float32)
    return (2.0 * flips - 1.0).astype(jnp.bfloat16)


def draw_probe_out(key, part):
    key = jax.random.fold_in(key, 23)
    flips = jax.random.bernoulli(key, 0.5, (FF, D)).astype(jnp.float32)
    return (2.0 * flips - 1.0).astype(jnp.bfloat16)


def level_of(key, shape, pieces, smallest, top_value):
    loudness, own = 1.0, jax.random.fold_in(key, 6)
    for position, shards_of in pieces:
        steps = jnp.exp(jax.random.uniform(jax.random.fold_in(own, position), (shards_of,), jnp.float32, smallest / len(pieces), top_value / len(pieces)))
        loudness = loudness * jnp.repeat(steps, shape[position] // shards_of).reshape([-1 if axis == position else 1 for axis in range(len(shape))])
    return loudness


def noise(rng, shape, scale, reach, pieces=(), dtype=jnp.bfloat16):
    gain = level_of(rng, shape, pieces, -0.22, 0.18) if pieces else 1.0
    values = jax.random.normal(rng, shape, jnp.float32) * scale * gain
    return jnp.minimum(jnp.maximum(values, -reach), reach).astype(dtype)


def setup_inputs(seed: int = 0) -> dict:
    seeds = jax.random.split(jax.random.key(seed), 7)
    return {
        "inputs": noise(seeds[0], (TOKENS, D), 1.0, 6.0, ((1, 16),)),
        "target": noise(seeds[1], (TOKENS, D), 1.0, 6.0, ((1, 16),)),
        "w_in": noise(seeds[2], (D, FF), D ** -0.5, 0.0625, ((0, 16), (1, 16))),
        "w_out": noise(seeds[3], (FF, D), FF ** -0.5, 0.046875, ((0, 16), (1, 16))),
        "probe_in": draw_probe_in(jax.random.fold_in(seeds[6], 71), 0),
        "probe_out": draw_probe_out(jax.random.fold_in(seeds[6], 71), 0),
    }


def gelu_parts(pre):
    cdf = 0.5 * (1.0 + lax.erf(pre * 0.7071067811865476))
    dens = jnp.exp(-0.5 * pre * pre) * 0.3989422804014327
    return pre * cdf, cdf + pre * dens, dens * (2.0 - pre * pre)


def reference(inputs, target, w_in, w_out, probe_in, probe_out):
    scale_in = D ** -0.5
    scale_out = FF ** -0.5
    loss_scale = TOKENS ** -0.5
    pre = jnp.dot(inputs, w_in, preferred_element_type=jnp.float32)
    pre_t = scale_in * jnp.dot(inputs, probe_in, preferred_element_type=jnp.float32)
    value, slope, bend = gelu_parts(pre)
    act = value.astype(jnp.bfloat16)
    act_t = (slope * pre_t).astype(jnp.bfloat16)
    out = jnp.dot(act, w_out, preferred_element_type=jnp.float32)
    out_t = jnp.dot(act_t, w_out, preferred_element_type=jnp.float32) + scale_out * jnp.dot(act, probe_out, preferred_element_type=jnp.float32)
    resid = (loss_scale * (out - target.astype(jnp.float32))).astype(jnp.bfloat16)
    resid_t = (loss_scale * out_t).astype(jnp.bfloat16)
    hess_out = jnp.dot(act_t.T, resid, preferred_element_type=jnp.float32) + jnp.dot(act.T, resid_t, preferred_element_type=jnp.float32)
    back = jnp.dot(resid, w_out.T, preferred_element_type=jnp.float32)
    back_t = jnp.dot(resid_t, w_out.T, preferred_element_type=jnp.float32) + scale_out * jnp.dot(resid, probe_out.T, preferred_element_type=jnp.float32)
    curv = (back_t * slope + back * bend * pre_t).astype(jnp.bfloat16)
    hess_in = jnp.dot(inputs.T, curv, preferred_element_type=jnp.float32)
    return hess_in.astype(jnp.bfloat16), hess_out.astype(jnp.bfloat16)
```

```python
import jax
import jax.numpy as jnp
from jax import lax
from jax.experimental import pallas as pl
from jax.experimental.pallas import tpu as pltpu
from jax.sharding import PartitionSpec as P

D = 9216
FF = 18432
MESH = pl.DeviceIdType.MESH
F32 = jnp.float32
BF16 = jnp.bfloat16

PARTS = 4
STAGES = 11

CORE, Y, Z, SHARE_Y, SHARE_CORE = 0, 1, 2, 3, 4
BACK = 5
X, L, SHARE_L, SHARE_X = 10, 11, 12, 13
KINDS = 14


def gelu_parts(pre):
    cdf = 0.5 * (1.0 + lax.erf(pre * 0.7071067811865476))
    dens = jnp.exp(-0.5 * pre * pre) * 0.3989422804014327
    return (pre * cdf, cdf + pre * dens, dens * (2.0 - pre * pre))


def dot(left, right):
    return jnp.dot(left, right, preferred_element_type=F32)


def kernel(
    inputs, target, w_in, w_out, probe_in, probe_out, hess_in, hess_out,
    x_v, tgt_v, w_in_v, w_out_v, p_in_v, p_out_v, w_out_t, p_out_t, x_t,
    ship, got_core, ship_y, got_y, ship_z, got_z, act, slope_v, bend_v, curv,
    ship_x, got_x, ship_l, got_l, resid, load_sem, send_sem, recv_sem,
):
    row, col = lax.axis_index("row"), lax.axis_index("col")
    core, hi, y = lax.rem(row, 2), lax.rem(row // 2, 2), row // 4
    x, low = col // 4, lax.rem(col, 4)
    tokens = x_v.shape[0]
    part = tokens // PARTS
    rows = part // 8
    ff, width = w_out_v.shape
    scale_in, scale_out, loss_scale = D ** (-0.5), FF ** (-0.5), tokens ** (-0.5)

    def at(y_, hi_, core_, x_, low_):
        return {"row": (y_ * 2 + hi_) * 2 + core_, "col": x_ * 4 + low_}

    def turn(i, d):
        return lax.rem(i + d, 4)

    twin = at(y, hi, 1 - core, x, low)
    far = at(y, 1 - hi, core, x, low)
    along_y = [at(turn(y, d), hi, core, x, low) for d in (1, 2, 3)]
    along_x = [at(y, hi, core, turn(x, d), low) for d in (1, 2, 3)]
    along_l = [at(y, hi, core, x, turn(low, d)) for d in (1, 2, 3)]

    loads = [
        pltpu.make_async_copy(src, dst, load_sem.at[k])
        for k, (src, dst) in enumerate(
            [(inputs, x_v), (w_in, w_in_v), (probe_in, p_in_v), (w_out, w_out_v), (probe_out, p_out_v), (target, tgt_v)]
        )
    ]
    for load in loads:
        load.start()

    barrier = pltpu.get_barrier_semaphore()
    peers = [twin, far, *along_y, *along_x, *along_l]
    for peer in peers:
        pl.semaphore_signal(barrier, 1, device_id=peer, device_id_type=MESH)
    pl.semaphore_wait(barrier, len(peers))

    def copies(kind, t, triples):
        return [
            pltpu.make_async_remote_copy(
                src, dst, send_sem.at[kind, t, k], recv_sem.at[kind, t, k], device_id=device, device_id_type=MESH
            )
            for k, (src, dst, device) in enumerate(triples)
        ]

    def core_copies(b, t):
        return copies(CORE + b * BACK, t, [(ship.at[b, t, 1 - core], got_core.at[b, t], twin)])

    def y_copies(b, t):
        return copies(
            Y + b * BACK, t, [(ship_y.at[b, t, turn(y, d)], got_y.at[b, t, d - 1], along_y[d - 1]) for d in (1, 2, 3)]
        )

    def z_copies(b, t):
        return copies(Z + b * BACK, t, [(ship_z.at[b, t], got_z.at[b, t], far)])

    def share_y_copies(b, t):
        held = curv if b else act
        return copies(SHARE_Y + b * BACK, t, [(held.at[t, core, y], held.at[t, core, y], peer) for peer in along_y])

    def share_core_copies(b, t):
        held = curv if b else act
        return copies(SHARE_CORE + b * BACK, t, [(held.at[t, core], held.at[t, core], twin)])

    def x_copies(t):
        return copies(X, t, [(ship_x.at[t, turn(x, d)], got_x.at[t, d - 1], along_x[d - 1]) for d in (1, 2, 3)])

    def l_copies(t):
        return copies(L, t, [(ship_l.at[t, turn(low, d)], got_l.at[t, d - 1], along_l[d - 1]) for d in (1, 2, 3)])

    def share_l_copies(t):
        return copies(SHARE_L, t, [(resid.at[t, x, low], resid.at[t, x, low], peer) for peer in along_l])

    def share_x_copies(t):
        return copies(SHARE_X, t, [(resid.at[t, x], resid.at[t, x], peer) for peer in along_x])

    def start(some):
        for copy in some:
            copy.start()

    def wait(some):
        for copy in some:
            copy.wait()

    def wide(ref):
        return ref[...].astype(F32)

    def put_partials(b, t, first, second):
        shape = (2, 4, rows, ff)
        ship[b, t, :, :, :rows, :] = first.astype(BF16).reshape(shape)
        ship[b, t, :, :, rows:, :] = second.astype(BF16).reshape(shape)
        start(core_copies(b, t))

    def pre_partials(t):
        some = x_v[pl.ds(pl.multiple_of(t * part, part), part), :]
        put_partials(0, t, dot(some, w_in_v[...]), dot(some, p_in_v[...]))

    def sum_cores(b, t):
        wait(core_copies(b, t))
        ship_y[b, t] = (wide(ship.at[b, t, core]) + wide(got_core.at[b, t])).astype(BF16)
        start(y_copies(b, t))

    def sum_y(b, t):
        wait(y_copies(b, t))
        total = wide(ship_y.at[b, t, y])
        for k in range(3):
            total += wide(got_y.at[b, t, k])
        ship_z[b, t] = total.astype(BF16)
        start(z_copies(b, t))

    def sum_z(b, t):
        wait(z_copies(b, t))
        total = wide(ship_z.at[b, t]) + wide(got_z.at[b, t])
        return total[:rows], total[rows:]

    def activate(t):
        pre, pre_t = sum_z(0, t)
        pre_t = scale_in * pre_t
        value, slope, bend = gelu_parts(pre)
        act[t, core, y, :rows, :] = value.astype(BF16)
        act[t, core, y, rows:, :] = (slope * pre_t).astype(BF16)
        start(share_y_copies(0, t))
        slope_v[t] = slope
        bend_v[t] = bend * pre_t

    def pass_on(b, t):
        wait(share_y_copies(b, t))
        start(share_core_copies(b, t))

    def out_partials(t):
        wait(share_core_copies(0, t))
        some = act[t, :, :, :rows, :].reshape(part, ff)
        some_t = act[t, :, :, rows:, :].reshape(part, ff)
        out = dot(some, w_out_v[...])
        out_t = dot(some_t, w_out_v[...]) + scale_out * dot(some, p_out_v[...])
        ship_x[t, 0:2] = out.astype(BF16).reshape(2, part // 2, width)
        ship_x[t, 2:4] = out_t.astype(BF16).reshape(2, part // 2, width)
        start(x_copies(t))

    def sum_x(t):
        wait(x_copies(t))
        total = wide(ship_x.at[t, x])
        for k in range(3):
            total += wide(got_x.at[t, k])
        ship_l[t] = total.astype(BF16).reshape(4, rows, width)
        start(l_copies(t))

    def residuals(t):
        wait(l_copies(t))
        total = wide(ship_l.at[t, low])
        for k in range(3):
            total += wide(got_l.at[t, k])
        first = t * part + lax.rem(x, 2) * (part // 2) + low * rows
        wanted = tgt_v[pl.ds(pl.multiple_of(first, rows), rows), :].astype(F32)
        wanted = wanted * (x < 2).astype(F32)
        resid[t, x, low] = (loss_scale * (total - wanted)).astype(BF16)
        start(share_l_copies(t))

    def pass_on_x(t):
        wait(share_l_copies(t))
        start(share_x_copies(t))

    def back_partials(t):
        wait(share_x_copies(t))
        some = resid[t, 0:2].reshape(part, width)
        some_t = resid[t, 2:4].reshape(part, width)
        back = dot(some, w_out_t[...])
        back_t = dot(some_t, w_out_t[...]) + scale_out * dot(some, p_out_t[...])
        put_partials(1, t, back, back_t)

    def curvature(t):
        back, back_t = sum_z(1, t)
        curv[t, core, y] = (back_t * slope_v[t] + back * bend_v[t]).astype(BF16)
        start(share_y_copies(1, t))

    def second_loads():
        for load in loads[3:]:
            load.wait()

    def transpose():
        for i in range(ff // 128):
            w_out_t[:, i * 128 : (i + 1) * 128] = w_out_v[i * 128 : (i + 1) * 128, :].T
            p_out_t[:, i * 128 : (i + 1) * 128] = p_out_v[i * 128 : (i + 1) * 128, :].T
        for i in range(tokens // 128):
            x_t[:, i * 128 : (i + 1) * 128] = x_v[i * 128 : (i + 1) * 128, :].T

    def outer_out():
        one = resid[:, 0:2].reshape(tokens, width)
        one_t = resid[:, 2:4].reshape(tokens, width)

        @pl.loop(0, ff // 384)
        def _(i):
            cols = pl.ds(pl.multiple_of(i * 384, 384), 384)
            some = act[:, :, :, :rows, cols].reshape(tokens, 384)
            some_t = act[:, :, :, rows:, cols].reshape(tokens, 384)
            hess_out[cols, :] = (dot(some_t.T, one) + dot(some.T, one_t)).astype(BF16)

    steps = [
        (0, lambda t: pre_partials(t)),
        (10, lambda t: pass_on(1, t)),
        (7, lambda t: back_partials(t)),
        (3, lambda t: pass_on(0, t)),
        (9, lambda t: curvature(t)),
        (8, lambda t: sum_y(1, t)),
        (6, lambda t: pass_on_x(t)),
        (5, lambda t: residuals(t)),
        (4, lambda t: sum_x(t)),
        (2, lambda t: activate(t)),
        (1, lambda t: sum_y(0, t)),
        (10, lambda t: wait(share_core_copies(1, t))),
        (7, lambda t: sum_cores(1, t)),
        (3, lambda t: out_partials(t)),
        (0, lambda t: sum_cores(0, t)),
    ]

    for load in loads[:3]:
        load.wait()

    def tick(i, _):
        pl.when(i == 1)(second_loads)
        pl.when(i == 4)(transpose)
        for stage, step in steps:
            t = i - stage

            @pl.when((t >= 0) & (t < PARTS))
            def _(step=step, t=t):
                step(t)

        pl.when(i == STAGES)(outer_out)
        return 0

    lax.fori_loop(0, STAGES + PARTS - 1, tick, 0)

    total = curv[...].reshape(tokens, ff)

    @pl.loop(0, width // 192)
    def _(i):
        cut = pl.ds(pl.multiple_of(i * 192, 192), 192)
        hess_in[cut, :] = dot(x_t[cut, :], total).astype(BF16)


def on_device(inputs, target, w_in, w_out, probe_in, probe_out):
    tokens, width = inputs.shape
    ff = w_in.shape[1]
    part = tokens // PARTS
    rows = part // 8
    two = 2 * rows
    n = PARTS
    return pl.pallas_call(
        kernel,
        out_shape=(jax.ShapeDtypeStruct((width, ff), BF16), jax.ShapeDtypeStruct((ff, width), BF16)),
        in_specs=[pl.BlockSpec(memory_space=pl.ANY)] * 6,
        out_specs=(pl.BlockSpec(memory_space=pltpu.VMEM),) * 2,
        scratch_shapes=[
            pltpu.VMEM((tokens, width), BF16),
            pltpu.VMEM((tokens, width), BF16),
            pltpu.VMEM((width, ff), BF16),
            pltpu.VMEM((ff, width), BF16),
            pltpu.VMEM((width, ff), BF16),
            pltpu.VMEM((ff, width), BF16),
            pltpu.VMEM((width, ff), BF16),
            pltpu.VMEM((width, ff), BF16),
            pltpu.VMEM((width, tokens), BF16),
            pltpu.VMEM((2, n, 2, 4, two, ff), BF16),
            pltpu.VMEM((2, n, 4, two, ff), BF16),
            pltpu.VMEM((2, n, 4, two, ff), BF16),
            pltpu.VMEM((2, n, 3, two, ff), BF16),
            pltpu.VMEM((2, n, two, ff), BF16),
            pltpu.VMEM((2, n, two, ff), BF16),
            pltpu.VMEM((n, 2, 4, two, ff), BF16),
            pltpu.VMEM((n, rows, ff), F32),
            pltpu.VMEM((n, rows, ff), F32),
            pltpu.VMEM((n, 2, 4, rows, ff), BF16),
            pltpu.VMEM((n, 4, part // 2, width), BF16),
            pltpu.VMEM((n, 3, part // 2, width), BF16),
            pltpu.VMEM((n, 4, rows, width), BF16),
            pltpu.VMEM((n, 3, rows, width), BF16),
            pltpu.VMEM((n, 4, 4, rows, width), BF16),
            pltpu.SemaphoreType.DMA((6,)),
            pltpu.SemaphoreType.DMA((KINDS, n, 3)),
            pltpu.SemaphoreType.DMA((KINDS, n, 3)),
        ],
        compiler_params=pltpu.CompilerParams(
            collective_id=0, has_side_effects=True, vmem_limit_bytes=56 * 1024 * 1024
        ),
        cost_estimate=pl.CostEstimate(
            flops=22 * tokens * width * ff, bytes_accessed=12 * width * ff, transcendentals=0
        ),
    )(inputs, target, w_in, w_out, probe_in, probe_out)


def solution(mesh):
    placed = (
        P(None, "row"),
        P(None, "row"),
        P("row", "col"),
        P("col", "row"),
        P("row", "col"),
        P("col", "row"),
    )
    return jax.shard_map(
        on_device,
        mesh=mesh,
        in_specs=placed,
        out_specs=(P("row", "col"), P("col", "row")),
        check_vma=False,
    )
```

```python
import jax
import jax.numpy as jnp
from jax import lax
from jax.experimental import pallas as pl
from jax.experimental.pallas import tpu as pltpu
from jax.sharding import PartitionSpec as P

D = 9216
FF = 18432
MESH = pl.DeviceIdType.MESH
F32 = jnp.float32
BF16 = jnp.bfloat16

PARTS = 4
GROUP = 128
PERIOD = 3.7

CORE, Y, Z, SHARE_Y, SHARE_CORE = 0, 1, 2, 3, 4
BACK = 5
X, L, SHARE_L, SHARE_X = 10, 11, 12, 13
FIRST = (0, 1, 4, 5, 8, 12, 13, 16, 17, 20, 24, 27, 30, 33)
SEMS = 36


def gelu_parts(pre):
    cdf = 0.5 * (1.0 + lax.erf(pre * 0.7071067811865476))
    dens = jnp.exp(-0.5 * pre * pre) * 0.3989422804014327
    return (pre * cdf, cdf + pre * dens, dens * (2.0 - pre * pre))


def dot(left, right):
    return jnp.dot(left, right, preferred_element_type=F32)


def kernel(
    inputs, target, w_in, w_out, probe_in, probe_out, hess_in, hess_out,
    x_t, tgt_t, tgt_v, w_in_v, p_in_v, w_out_t, p_out_t, w_out_v, p_out_v, resid_t, resid_tt, outer,
    ship, got_core, ship_y, got_y, ship_z, got_z, kept, act, slope_v, bend_v, curv,
    ship_x, got_x, ship_l, got_l, resid, load_sem, send_sem, recv_sem,
):
    row, col = lax.axis_index("row"), lax.axis_index("col")
    core, hi, y = lax.rem(row, 2), lax.rem(row // 2, 2), row // 4
    x, low = col // 4, lax.rem(col, 4)
    tokens = tgt_v.shape[0]
    part = tokens // PARTS
    rows, per = part // 8, GROUP // part
    ff, width = w_out_v.shape
    scale_in, scale_out, loss_scale = D ** (-0.5), FF ** (-0.5), tokens ** (-0.5)

    def at(y_, hi_, core_, x_, low_):
        return {"row": (y_ * 2 + hi_) * 2 + core_, "col": x_ * 4 + low_}

    def turn(i, d):
        return lax.rem(i + d, 4)

    twin = at(y, hi, 1 - core, x, low)
    far = at(y, 1 - hi, core, x, low)
    along_y = [at(turn(y, d), hi, core, x, low) for d in (1, 2, 3)]
    along_x = [at(y, hi, core, turn(x, d), low) for d in (1, 2, 3)]
    along_l = [at(y, hi, core, x, turn(low, d)) for d in (1, 2, 3)]

    loads = [
        pltpu.make_async_copy(src, dst, load_sem.at[k])
        for k, (src, dst) in enumerate(
            [(inputs, x_t), (w_in, w_in_v), (probe_in, p_in_v), (w_out, w_out_t), (probe_out, p_out_t), (target, tgt_t)]
        )
    ]
    for load in loads:
        load.start()

    barrier = pltpu.get_barrier_semaphore()
    peers = [twin, far, *along_y, *along_x, *along_l]
    for peer in peers:
        pl.semaphore_signal(barrier, 1, device_id=peer, device_id_type=MESH)

    def copies(kind, t, triples, first=0):
        return [
            pltpu.make_async_remote_copy(
                src, dst, send_sem.at[t, FIRST[kind] + k], recv_sem.at[t, FIRST[kind] + k], device_id=device, device_id_type=MESH
            )
            for k, (src, dst, device) in enumerate(triples, first)
        ]

    def core_copies(b, t):
        return copies(CORE + b * BACK, t, [(ship.at[b, t, 1 - core], got_core.at[b, t], twin)])

    def y_copies(b, t):
        return copies(
            Y + b * BACK, t, [(ship_y.at[b, t, turn(y, d)], got_y.at[b, t, d - 1], along_y[d - 1]) for d in (1, 2, 3)]
        )

    def z_copies(b, t):
        return copies(Z + b * BACK, t, [(ship_z.at[b, t], got_z.at[b, t], far)])

    def share_y_copies(b, t):
        held = curv if b else act
        return copies(SHARE_Y + b * BACK, t, [(held.at[t, core, y], held.at[t, core, y], peer) for peer in along_y])

    def share_core_copy(b, t, d):
        piece = (curv if b else act).at[t, core, turn(y, 4 - d)]
        return copies(SHARE_CORE + b * BACK, t, [(piece, piece, twin)], d)[0]

    def share_core_copies(b, t):
        return [share_core_copy(b, t, d) for d in (0, 1, 2, 3)]

    def x_copies(t):
        return copies(X, t, [(ship_x.at[t, turn(x, d)], got_x.at[t, d - 1], along_x[d - 1]) for d in (1, 2, 3)])

    def l_copies(t):
        return copies(L, t, [(ship_l.at[t, turn(low, d)], got_l.at[t, d - 1], along_l[d - 1]) for d in (1, 2, 3)])

    def share_l_copies(t):
        return copies(SHARE_L, t, [(resid.at[t, x, low], resid.at[t, x, low], peer) for peer in along_l])

    def share_x_copies(t):
        return copies(SHARE_X, t, [(resid.at[t, x], resid.at[t, x], peer) for peer in along_x])

    def start(some):
        for copy in some[1:2] + some[:1] + some[2:]:
            copy.start()

    def wait(some):
        for copy in some:
            copy.wait()

    def wide(ref):
        return ref[...].astype(F32)

    def flat(value):
        return value.astype(F32).reshape(-1, value.shape[-1]).astype(BF16)

    def put(b, t, which, partial):
        ship[b, t, :, :, which] = partial.reshape(2, 4, rows, ff).astype(BF16)

    def pre_partials(g):
        some = x_t[:, pl.ds(pl.multiple_of(g * GROUP, GROUP), GROUP)].T
        parts = pl.ds(g * per, per)
        ship[0, parts, :, :, 0] = dot(some, w_in_v[...]).reshape(per, 2, 4, rows, ff).astype(BF16)
        ship[0, parts, :, :, 1] = dot(some, p_in_v[...]).reshape(per, 2, 4, rows, ff).astype(BF16)

    def sum_cores(b, t):
        wait(core_copies(b, t))
        ship_y[b, t] = (wide(ship.at[b, t, core]) + wide(got_core.at[b, t])).astype(BF16)
        start(y_copies(b, t))

    def sum_y(b, t):
        wait(y_copies(b, t))
        total = wide(ship.at[b, t, core, y]) + wide(got_core.at[b, t, y])
        for k in range(3):
            total += wide(got_y.at[b, t, k])
        ship_z[b, t] = total.astype(BF16)
        kept[b, t] = total
        start(z_copies(b, t))

    def sum_z(b, t):
        wait(z_copies(b, t))
        total = kept[b, t] + wide(got_z.at[b, t])
        return total[0], total[1]

    def activate(t):
        pre, pre_t = sum_z(0, t)
        pre_t = scale_in * pre_t
        value, slope, bend = gelu_parts(pre)
        act[t, core, y, 0] = value.astype(BF16)
        act[t, core, y, 1] = (slope * pre_t).astype(BF16)
        start(share_y_copies(0, t))
        share_core_copy(0, t, 0).start()
        slope_v[t] = slope
        bend_v[t] = bend * pre_t

    def pass_on(b, t):
        arrive = share_y_copies(b, t)
        for d in (1, 3, 2):
            arrive[d - 1].wait()
            share_core_copy(b, t, d).start()

    def out_partials(t):
        wait(share_core_copies(0, t))
        some, some_t = flat(act[t, :, :, 0]), flat(act[t, :, :, 1])
        out = dot(some, w_out_v[...])
        out_t = dot(some_t, w_out_v[...]) + scale_out * dot(some, p_out_v[...])
        ship_x[t, 0:2] = out.reshape(2, 4, rows, width).astype(BF16)
        ship_x[t, 2:4] = out_t.reshape(2, 4, rows, width).astype(BF16)
        start(x_copies(t))

    def sum_x(t):
        wait(x_copies(t))
        total = wide(ship_x.at[t, x])
        for k in range(3):
            total += wide(got_x.at[t, k])
        ship_l[t] = total.astype(BF16)
        start(l_copies(t))

    def residuals(t):
        wait(l_copies(t))
        total = wide(ship_x.at[t, x, low])
        for k in range(3):
            total += wide(got_x.at[t, k, low])
        for k in range(3):
            total += wide(got_l.at[t, k])
        first = t * part + lax.rem(x, 2) * (part // 2) + low * rows
        wanted = tgt_v[pl.ds(pl.multiple_of(first, rows), rows), :]
        wanted = wanted * (x < 2).astype(F32)
        resid[t, x, low] = (loss_scale * (total - wanted)).astype(BF16)
        start(share_l_copies(t))

    def pass_on_x(t):
        wait(share_l_copies(t))
        start(share_x_copies(t))

    def back_partials(t):
        wait(share_x_copies(t))
        some, some_t = flat(resid[t, 0:2]), flat(resid[t, 2:4])
        back = dot(some, w_out_t[...])
        back_t = dot(some_t, w_out_t[...]) + scale_out * dot(some, p_out_t[...])
        put(1, t, 0, back)
        put(1, t, 1, back_t)
        start(core_copies(1, t))

    def curvature(t):
        back, back_t = sum_z(1, t)
        curv[t, core, y] = (back_t * slope_v[t] + back * bend_v[t]).astype(BF16)
        start(share_y_copies(1, t))
        share_core_copy(1, t, 0).start()

    def turn_w():
        loads[3].wait()
        for i in range(ff // 128):
            w_out_v[i * 128 : (i + 1) * 128, :] = w_out_t[:, i * 128 : (i + 1) * 128].T

    def turn_p():
        loads[4].wait()
        for i in range(ff // 128):
            p_out_v[i * 128 : (i + 1) * 128, :] = p_out_t[:, i * 128 : (i + 1) * 128].T

    def turn_target():
        loads[5].wait()
        for i in range(tokens // 128):
            tgt_v[i * 128 : (i + 1) * 128, :] = tgt_t[:, i * 128 : (i + 1) * 128].T.astype(F32)

    def outer_out():
        resid_t[...] = flat(resid[:, 0:2]).T
        resid_tt[...] = flat(resid[:, 2:4]).T

        @pl.loop(0, ff // 384)
        def _(i):
            cols = pl.ds(pl.multiple_of(i * 384, 384), 384)
            some, some_t = flat(act[:, :, :, 0, :, cols]), flat(act[:, :, :, 1, :, cols])
            hess_out[:, cols] = (dot(resid_t[...], some_t) + dot(resid_tt[...], some)).astype(BF16)

    def outer_in(first, last, add):
        some = flat(curv[first:last])

        @pl.loop(0, width // 192)
        def _(i):
            cut = pl.ds(pl.multiple_of(i * 192, 192), 192)
            product = dot(x_t[cut, first * part : last * part], some)
            if add:
                hess_in[cut, :] = (outer[cut, :] + product).astype(BF16)
            else:
                outer[cut, :] = product

    def next_partials(t):
        if per == 1:
            pre_partials(t)
        else:
            pl.when(lax.rem(t, per) == 0)(lambda: pre_partials(t // per))

    steps = [
        (-1.5, next_partials),
        (0.0, lambda t: start(core_copies(0, t))),
        (5.3, lambda t: sum_cores(0, t)),
        (11.2, lambda t: sum_y(0, t)),
        (19.0, activate),
        (25.7, lambda t: pass_on(0, t)),
        (28.4, out_partials),
        (34.5, sum_x),
        (39.7, residuals),
        (45.3, pass_on_x),
        (52.2, back_partials),
        (54.0, lambda t: sum_cores(1, t)),
        (60.3, lambda t: sum_y(1, t)),
        (71.4, curvature),
        (78.0, lambda t: pass_on(1, t)),
        (83.3, lambda t: wait(share_core_copies(1, t))),
    ]
    order = sorted(((when % PERIOD, int(when // PERIOD), step) for when, step in steps), key=lambda entry: entry[0])
    last_tick = max(stage for _, stage, _ in order)
    back_tick = int(52.2 // PERIOD) + PARTS - 1

    for load in loads[:3]:
        load.wait()
    pre_partials(0)
    pl.semaphore_wait(barrier, len(peers))

    def tick(i, _):
        for _, stage, step in order:
            t = i - stage

            @pl.when((t >= max(0, -stage)) & (t < PARTS))
            def _(step=step, t=t):
                step(t)

        pl.when(i == 0)(turn_w)
        pl.when(i == 1)(turn_p)
        pl.when(i == 2)(turn_target)
        pl.when(i == back_tick)(outer_out)
        pl.when(i == last_tick + PARTS - per - 1)(lambda: outer_in(0, PARTS - per, False))
        return 0

    lax.fori_loop(0, last_tick + PARTS, tick, 0)

    outer_in(PARTS - per, PARTS, True)


def on_device(inputs, target, w_in, w_out, probe_in, probe_out):
    tokens, width = inputs.shape
    ff = w_in.shape[1]
    part = tokens // PARTS
    rows = part // 8
    n = PARTS
    hess_in, hess_out = pl.pallas_call(
        kernel,
        out_shape=(pltpu.VMEM((width, ff), BF16), pltpu.VMEM((width, ff), BF16)),
        in_specs=[pl.BlockSpec(memory_space=pl.ANY)] * 6,
        out_specs=(pl.BlockSpec(memory_space=pltpu.VMEM),) * 2,
        scratch_shapes=[
            pltpu.VMEM((width, tokens), BF16),
            pltpu.VMEM((width, tokens), BF16),
            pltpu.VMEM((tokens, width), F32),
            pltpu.VMEM((width, ff), BF16),
            pltpu.VMEM((width, ff), BF16),
            pltpu.VMEM((width, ff), BF16),
            pltpu.VMEM((width, ff), BF16),
            pltpu.VMEM((ff, width), BF16),
            pltpu.VMEM((ff, width), BF16),
            pltpu.VMEM((width, tokens), BF16),
            pltpu.VMEM((width, tokens), BF16),
            pltpu.VMEM((width, ff), F32),
            pltpu.VMEM((2, n, 2, 4, 2, rows, ff), BF16),
            pltpu.VMEM((2, n, 4, 2, rows, ff), BF16),
            pltpu.VMEM((2, n, 4, 2, rows, ff), BF16),
            pltpu.VMEM((2, n, 3, 2, rows, ff), BF16),
            pltpu.VMEM((2, n, 2, rows, ff), BF16),
            pltpu.VMEM((2, n, 2, rows, ff), BF16),
            pltpu.VMEM((2, n, 2, rows, ff), F32),
            pltpu.VMEM((n, 2, 4, 2, rows, ff), BF16),
            pltpu.VMEM((n, rows, ff), F32),
            pltpu.VMEM((n, rows, ff), F32),
            pltpu.VMEM((n, 2, 4, rows, ff), BF16),
            pltpu.VMEM((n, 4, 4, rows, width), BF16),
            pltpu.VMEM((n, 3, 4, rows, width), BF16),
            pltpu.VMEM((n, 4, rows, width), BF16),
            pltpu.VMEM((n, 3, rows, width), BF16),
            pltpu.VMEM((n, 4, 4, rows, width), BF16),
            pltpu.SemaphoreType.DMA((6,)),
            pltpu.SemaphoreType.DMA((n, SEMS)),
            pltpu.SemaphoreType.DMA((n, SEMS)),
        ],
        compiler_params=pltpu.CompilerParams(
            collective_id=0, has_side_effects=True, vmem_limit_bytes=56 * 1024 * 1024
        ),
        cost_estimate=pl.CostEstimate(
            flops=22 * tokens * width * ff, bytes_accessed=12 * width * ff, transcendentals=0
        ),
    )(inputs.T, target.T, w_in, w_out.T, probe_in, probe_out.T)
    return hess_in, hess_out.T


def solution(mesh):
    placed = (
        P(None, "row"),
        P(None, "row"),
        P("row", "col"),
        P("col", "row"),
        P("row", "col"),
        P("col", "row"),
    )
    return jax.shard_map(
        on_device,
        mesh=mesh,
        in_specs=placed,
        out_specs=(P("row", "col"), P("col", "row")),
        check_vma=False,
    )
```

```python
import jax
import jax.numpy as jnp
from jax import lax
from jax.experimental import pallas as pl
from jax.experimental.pallas import tpu as pltpu
from jax.sharding import PartitionSpec as P

D = 9216
FF = 18432
MESH = pl.DeviceIdType.MESH
F32 = jnp.float32
BF16 = jnp.bfloat16

PARTS = 4
GROUP = 128
PERIOD = 3.7

CORE, Y, Z, SHARE_Y, SHARE_CORE = 0, 1, 2, 3, 4
BACK = 5
X, L, SHARE_L, SHARE_X = 10, 11, 12, 13
FIRST = (0, 1, 4, 5, 8, 12, 13, 16, 17, 20, 24, 27, 30, 33)
SEMS = 36


def gelu_parts(pre):
    cdf = 0.5 * (1.0 + lax.erf(pre * 0.7071067811865476))
    dens = jnp.exp(-0.5 * pre * pre) * 0.3989422804014327
    return (pre * cdf, cdf + pre * dens, dens * (2.0 - pre * pre))


def dot(left, right):
    return jnp.dot(left, right, preferred_element_type=F32)


def kernel(
    inputs, target, w_in, w_out, probe_in, probe_out, hess_in, hess_out,
    x_t, tgt_t, tgt_v, w_in_v, p_in_v, w_out_t, p_out_t, w_out_v, p_out_v, resid_t, resid_tt, outer,
    ship, got_core, ship_y, got_y, ship_z, got_z, kept, act, slope_v, bend_v, curv,
    ship_x, got_x, ship_l, got_l, resid, load_sem, send_sem, recv_sem,
):
    row, col = lax.axis_index("row"), lax.axis_index("col")
    core, hi, y = lax.rem(row, 2), lax.rem(row // 2, 2), row // 4
    x, low = col // 4, lax.rem(col, 4)
    tokens = tgt_v.shape[0]
    part = tokens // PARTS
    rows, per = part // 8, GROUP // part
    ff, width = w_out_v.shape
    scale_in, scale_out, loss_scale = D ** (-0.5), FF ** (-0.5), tokens ** (-0.5)

    def at(y_, hi_, core_, x_, low_):
        return {"row": (y_ * 2 + hi_) * 2 + core_, "col": x_ * 4 + low_}

    def turn(i, d):
        return lax.rem(i + d, 4)

    twin = at(y, hi, 1 - core, x, low)
    far = at(y, 1 - hi, core, x, low)
    along_y = [at(turn(y, d), hi, core, x, low) for d in (1, 2, 3)]
    along_x = [at(y, hi, core, turn(x, d), low) for d in (1, 2, 3)]
    along_l = [at(y, hi, core, x, turn(low, d)) for d in (1, 2, 3)]

    loads = [
        pltpu.make_async_copy(src, dst, load_sem.at[k])
        for k, (src, dst) in enumerate(
            [(inputs, x_t), (w_in, w_in_v), (probe_in, p_in_v), (w_out, w_out_t), (probe_out, p_out_t), (target, tgt_t)]
        )
    ]
    for load in loads:
        load.start()

    barrier = pltpu.get_barrier_semaphore()
    peers = [twin, far, *along_y, *along_x, *along_l]
    for peer in peers:
        pl.semaphore_signal(barrier, 1, device_id=peer, device_id_type=MESH)

    def copies(kind, t, triples, first=0):
        return [
            pltpu.make_async_remote_copy(
                src, dst, send_sem.at[t, FIRST[kind] + k], recv_sem.at[t, FIRST[kind] + k], device_id=device, device_id_type=MESH
            )
            for k, (src, dst, device) in enumerate(triples, first)
        ]

    def core_copies(b, t):
        return copies(CORE + b * BACK, t, [(ship.at[b, t, 1 - core], got_core.at[b, t], twin)])

    def y_copies(b, t):
        return copies(
            Y + b * BACK, t, [(ship_y.at[b, t, turn(y, d)], got_y.at[b, t, d - 1], along_y[d - 1]) for d in (1, 2, 3)]
        )

    def z_copies(b, t):
        return copies(Z + b * BACK, t, [(ship_z.at[b, t], got_z.at[b, t], far)])

    def share_y_copies(b, t):
        held = curv if b else act
        return copies(SHARE_Y + b * BACK, t, [(held.at[t, core, y], held.at[t, core, y], peer) for peer in along_y])

    def share_core_copy(b, t, d):
        piece = (curv if b else act).at[t, core, turn(y, 4 - d)]
        return copies(SHARE_CORE + b * BACK, t, [(piece, piece, twin)], d)[0]

    def share_core_copies(b, t):
        return [share_core_copy(b, t, d) for d in (0, 1, 2, 3)]

    def x_copies(t):
        return copies(X, t, [(ship_x.at[t, turn(x, d)], got_x.at[t, d - 1], along_x[d - 1]) for d in (1, 2, 3)])

    def l_copies(t):
        return copies(L, t, [(ship_l.at[t, turn(low, d)], got_l.at[t, d - 1], along_l[d - 1]) for d in (1, 2, 3)])

    def share_l_copies(t):
        return copies(SHARE_L, t, [(resid.at[t, x, low], resid.at[t, x, low], peer) for peer in along_l])

    def share_x_copies(t):
        return copies(SHARE_X, t, [(resid.at[t, x], resid.at[t, x], peer) for peer in along_x])

    def start(some):
        for copy in some[1:2] + some[:1] + some[2:]:
            copy.start()

    def arrived(some):
        for copy in some:
            copy.wait_recv()

    def sent(some):
        for copy in some:
            copy.wait_send()

    def add_arrivals(total, some, refs):
        for k in (0, 2, 1):
            some[k].wait_recv()
            total += wide(refs(k))
        return total

    def wide(ref):
        return ref[...].astype(F32)

    def flat(value):
        return value.astype(F32).reshape(-1, value.shape[-1]).astype(BF16)

    def put(b, t, which, partial):
        ship[b, t, :, :, which] = partial.reshape(2, 4, rows, ff).astype(BF16)

    def pre_partials(g):
        some = x_t[:, pl.ds(pl.multiple_of(g * GROUP, GROUP), GROUP)].T
        parts = pl.ds(g * per, per)
        ship[0, parts, :, :, 0] = dot(some, w_in_v[...]).reshape(per, 2, 4, rows, ff).astype(BF16)
        ship[0, parts, :, :, 1] = dot(some, p_in_v[...]).reshape(per, 2, 4, rows, ff).astype(BF16)

    def sum_cores(b, t):
        before = core_copies(b, t)
        arrived(before)
        ship_y[b, t] = (wide(ship.at[b, t, core]) + wide(got_core.at[b, t])).astype(BF16)
        start(y_copies(b, t))
        sent(before)

    def sum_y(b, t):
        before = y_copies(b, t)
        total = wide(ship.at[b, t, core, y]) + wide(got_core.at[b, t, y])
        total = add_arrivals(total, before, lambda k: got_y.at[b, t, k])
        ship_z[b, t] = total.astype(BF16)
        kept[b, t] = total
        start(z_copies(b, t))
        sent(before)

    def sum_z(b, t):
        arrived(z_copies(b, t))
        total = kept[b, t] + wide(got_z.at[b, t])
        return total[0], total[1]

    def activate(t):
        pre, pre_t = sum_z(0, t)
        pre_t = scale_in * pre_t
        value, slope, bend = gelu_parts(pre)
        act[t, core, y, 0] = value.astype(BF16)
        act[t, core, y, 1] = (slope * pre_t).astype(BF16)
        start(share_y_copies(0, t))
        share_core_copy(0, t, 0).start()
        sent(z_copies(0, t))
        slope_v[t] = slope
        bend_v[t] = bend * pre_t

    def pass_on(b, t):
        arrive = share_y_copies(b, t)
        for d in (1, 3, 2):
            arrive[d - 1].wait_recv()
            share_core_copy(b, t, d).start()
        sent(arrive)

    def out_partials(t):
        before = share_core_copies(0, t)
        arrived(before)
        some, some_t = flat(act[t, :, :, 0]), flat(act[t, :, :, 1])
        out = dot(some, w_out_v[...])
        out_t = dot(some_t, w_out_v[...]) + scale_out * dot(some, p_out_v[...])
        ship_x[t, 0:2] = out.reshape(2, 4, rows, width).astype(BF16)
        ship_x[t, 2:4] = out_t.reshape(2, 4, rows, width).astype(BF16)
        start(x_copies(t))
        sent(before)

    def sum_x(t):
        before = x_copies(t)
        total = add_arrivals(wide(ship_x.at[t, x]), before, lambda k: got_x.at[t, k])
        ship_l[t] = total.astype(BF16)
        start(l_copies(t))
        sent(before)

    def residuals(t):
        before = l_copies(t)
        total = wide(ship_x.at[t, x, low])
        for k in range(3):
            total += wide(got_x.at[t, k, low])
        total = add_arrivals(total, before, lambda k: got_l.at[t, k])
        first = t * part + lax.rem(x, 2) * (part // 2) + low * rows
        wanted = tgt_v[pl.ds(pl.multiple_of(first, rows), rows), :]
        wanted = wanted * (x < 2).astype(F32)
        resid[t, x, low] = (loss_scale * (total - wanted)).astype(BF16)
        start(share_l_copies(t))
        sent(before)

    def pass_on_x(t):
        before = share_l_copies(t)
        arrived(before)
        start(share_x_copies(t))
        sent(before)

    def back_partials(t):
        before = share_x_copies(t)
        arrived(before)
        some, some_t = flat(resid[t, 0:2]), flat(resid[t, 2:4])
        back = dot(some, w_out_t[...])
        back_t = dot(some_t, w_out_t[...]) + scale_out * dot(some, p_out_t[...])
        put(1, t, 0, back)
        put(1, t, 1, back_t)
        start(core_copies(1, t))
        sent(before)

    def curvature(t):
        back, back_t = sum_z(1, t)
        curv[t, core, y] = (back_t * slope_v[t] + back * bend_v[t]).astype(BF16)
        start(share_y_copies(1, t))
        share_core_copy(1, t, 0).start()
        sent(z_copies(1, t))

    def whole_curv(t):
        before = share_core_copies(1, t)
        arrived(before)
        sent(before)

    def turn_w():
        loads[3].wait()
        for i in range(ff // 128):
            w_out_v[i * 128 : (i + 1) * 128, :] = w_out_t[:, i * 128 : (i + 1) * 128].T

    def turn_p():
        loads[4].wait()
        for i in range(ff // 128):
            p_out_v[i * 128 : (i + 1) * 128, :] = p_out_t[:, i * 128 : (i + 1) * 128].T

    def turn_target():
        loads[5].wait()
        for i in range(tokens // 128):
            tgt_v[i * 128 : (i + 1) * 128, :] = tgt_t[:, i * 128 : (i + 1) * 128].T.astype(F32)

    def outer_out():
        resid_t[...] = flat(resid[:, 0:2]).T
        resid_tt[...] = flat(resid[:, 2:4]).T

        @pl.loop(0, ff // 384)
        def _(i):
            cols = pl.ds(pl.multiple_of(i * 384, 384), 384)
            some, some_t = flat(act[:, :, :, 0, :, cols]), flat(act[:, :, :, 1, :, cols])
            hess_out[:, cols] = (dot(resid_t[...], some_t) + dot(resid_tt[...], some)).astype(BF16)

    def outer_in(first, last, add):
        some = flat(curv[first:last])

        @pl.loop(0, width // 192)
        def _(i):
            cut = pl.ds(pl.multiple_of(i * 192, 192), 192)
            product = dot(x_t[cut, first * part : last * part], some)
            if add:
                hess_in[cut, :] = (outer[cut, :] + product).astype(BF16)
            else:
                outer[cut, :] = product

    def next_partials(t):
        if per == 1:
            pre_partials(t)
        else:
            pl.when(lax.rem(t, per) == 0)(lambda: pre_partials(t // per))

    steps = [
        (-1.5, next_partials),
        (0.0, lambda t: start(core_copies(0, t))),
        (5.3, lambda t: sum_cores(0, t)),
        (11.2, lambda t: sum_y(0, t)),
        (19.0, activate),
        (25.7, lambda t: pass_on(0, t)),
        (28.4, out_partials),
        (34.5, sum_x),
        (39.7, residuals),
        (45.3, pass_on_x),
        (52.2, back_partials),
        (54.0, lambda t: sum_cores(1, t)),
        (60.3, lambda t: sum_y(1, t)),
        (71.4, curvature),
        (78.0, lambda t: pass_on(1, t)),
        (83.3, whole_curv),
    ]
    order = sorted(((when % PERIOD, int(when // PERIOD), step) for when, step in steps), key=lambda entry: entry[0])
    last_tick = max(stage for _, stage, _ in order)
    back_tick = int(52.2 // PERIOD) + PARTS - 1

    for load in loads[:3]:
        load.wait()
    pre_partials(0)
    pl.semaphore_wait(barrier, len(peers))

    def tick(i, _):
        for _, stage, step in order:
            t = i - stage

            @pl.when((t >= max(0, -stage)) & (t < PARTS))
            def _(step=step, t=t):
                step(t)

        pl.when(i == 0)(turn_w)
        pl.when(i == 1)(turn_p)
        pl.when(i == 2)(turn_target)
        pl.when(i == back_tick)(outer_out)
        pl.when(i == last_tick + PARTS - per - 1)(lambda: outer_in(0, PARTS - per, False))
        return 0

    lax.fori_loop(0, last_tick + PARTS, tick, 0)

    outer_in(PARTS - per, PARTS, True)


def on_device(inputs, target, w_in, w_out, probe_in, probe_out):
    tokens, width = inputs.shape
    ff = w_in.shape[1]
    part = tokens // PARTS
    rows = part // 8
    n = PARTS
    hess_in, hess_out = pl.pallas_call(
        kernel,
        out_shape=(pltpu.VMEM((width, ff), BF16), pltpu.VMEM((width, ff), BF16)),
        in_specs=[pl.BlockSpec(memory_space=pl.ANY)] * 6,
        out_specs=(pl.BlockSpec(memory_space=pltpu.VMEM),) * 2,
        scratch_shapes=[
            pltpu.VMEM((width, tokens), BF16),
            pltpu.VMEM((width, tokens), BF16),
            pltpu.VMEM((tokens, width), F32),
            pltpu.VMEM((width, ff), BF16),
            pltpu.VMEM((width, ff), BF16),
            pltpu.VMEM((width, ff), BF16),
            pltpu.VMEM((width, ff), BF16),
            pltpu.VMEM((ff, width), BF16),
            pltpu.VMEM((ff, width), BF16),
            pltpu.VMEM((width, tokens), BF16),
            pltpu.VMEM((width, tokens), BF16),
            pltpu.VMEM((width, ff), F32),
            pltpu.VMEM((2, n, 2, 4, 2, rows, ff), BF16),
            pltpu.VMEM((2, n, 4, 2, rows, ff), BF16),
            pltpu.VMEM((2, n, 4, 2, rows, ff), BF16),
            pltpu.VMEM((2, n, 3, 2, rows, ff), BF16),
            pltpu.VMEM((2, n, 2, rows, ff), BF16),
            pltpu.VMEM((2, n, 2, rows, ff), BF16),
            pltpu.VMEM((2, n, 2, rows, ff), F32),
            pltpu.VMEM((n, 2, 4, 2, rows, ff), BF16),
            pltpu.VMEM((n, rows, ff), F32),
            pltpu.VMEM((n, rows, ff), F32),
            pltpu.VMEM((n, 2, 4, rows, ff), BF16),
            pltpu.VMEM((n, 4, 4, rows, width), BF16),
            pltpu.VMEM((n, 3, 4, rows, width), BF16),
            pltpu.VMEM((n, 4, rows, width), BF16),
            pltpu.VMEM((n, 3, rows, width), BF16),
            pltpu.VMEM((n, 4, 4, rows, width), BF16),
            pltpu.SemaphoreType.DMA((6,)),
            pltpu.SemaphoreType.DMA((n, SEMS)),
            pltpu.SemaphoreType.DMA((n, SEMS)),
        ],
        compiler_params=pltpu.CompilerParams(
            collective_id=0, has_side_effects=True, vmem_limit_bytes=56 * 1024 * 1024
        ),
        cost_estimate=pl.CostEstimate(
            flops=22 * tokens * width * ff, bytes_accessed=12 * width * ff, transcendentals=0
        ),
    )(inputs.T, target.T, w_in, w_out.T, probe_in, probe_out.T)
    return hess_in, hess_out.T


def solution(mesh):
    placed = (
        P(None, "row"),
        P(None, "row"),
        P("row", "col"),
        P("col", "row"),
        P("row", "col"),
        P("col", "row"),
    )
    return jax.shard_map(
        on_device,
        mesh=mesh,
        in_specs=placed,
        out_specs=(P("row", "col"), P("col", "row")),
        check_vma=False,
    )
```

```python
import jax
import jax.numpy as jnp
from jax import lax
from jax.experimental import pallas as pl
from jax.experimental.pallas import tpu as pltpu
from jax.sharding import PartitionSpec as P

D = 9216
FF = 18432
MESH = pl.DeviceIdType.MESH
F32 = jnp.float32
BF16 = jnp.bfloat16

PARTS = 4
GROUP = 128
PERIOD = 3.7

CORE, Y, Z, SHARE_Y, SHARE_CORE = 0, 1, 2, 3, 4
BACK = 5
X, L, SHARE_L, SHARE_X = 10, 11, 12, 13
FIRST = (0, 1, 4, 5, 8, 12, 13, 16, 17, 20, 24, 27, 30, 33)
SEMS = 36


def gelu_parts(pre):
    cdf = 0.5 * (1.0 + lax.erf(pre * 0.7071067811865476))
    dens = jnp.exp(-0.5 * pre * pre) * 0.3989422804014327
    return (pre * cdf, cdf + pre * dens, dens * (2.0 - pre * pre))


def dot(left, right):
    return jnp.dot(left, right, preferred_element_type=F32)


def kernel(
    inputs, target, w_in, w_out, probe_in, probe_out, hess_in, hess_out,
    x_t, tgt_t, tgt_v, w_in_v, p_in_v, w_out_t, p_out_t, w_out_v, p_out_v, resid_t, resid_tt, outer,
    ship, got_core, ship_y, got_y, ship_z, got_z, kept, act, slope_v, bend_v, curv,
    ship_x, got_x, ship_l, got_l, resid, load_sem, send_sem, recv_sem,
):
    row, col = lax.axis_index("row"), lax.axis_index("col")
    core, hi, y = lax.rem(row, 2), lax.rem(row // 2, 2), row // 4
    x, low = col // 4, lax.rem(col, 4)
    tokens = tgt_v.shape[0]
    part = tokens // PARTS
    rows, per = part // 8, GROUP // part
    ff, width = w_out_v.shape
    scale_in, scale_out, loss_scale = D ** (-0.5), FF ** (-0.5), tokens ** (-0.5)

    def at(y_, hi_, core_, x_, low_):
        return {"row": (y_ * 2 + hi_) * 2 + core_, "col": x_ * 4 + low_}

    def turn(i, d):
        return lax.rem(i + d, 4)

    twin = at(y, hi, 1 - core, x, low)
    far = at(y, 1 - hi, core, x, low)
    along_y = [at(turn(y, d), hi, core, x, low) for d in (1, 2, 3)]
    along_x = [at(y, hi, core, turn(x, d), low) for d in (1, 2, 3)]
    along_l = [at(y, hi, core, x, turn(low, d)) for d in (1, 2, 3)]

    loads = [
        pltpu.make_async_copy(src, dst, load_sem.at[k])
        for k, (src, dst) in enumerate(
            [(inputs, x_t), (w_in, w_in_v), (probe_in, p_in_v), (w_out, w_out_t), (probe_out, p_out_t), (target, tgt_t)]
        )
    ]
    for load in loads:
        load.start()

    barrier = pltpu.get_barrier_semaphore()
    peers = [twin, far, *along_y, *along_x, *along_l]
    for peer in peers:
        pl.semaphore_signal(barrier, 1, device_id=peer, device_id_type=MESH)

    def copies(kind, t, triples, first=0):
        return [
            pltpu.make_async_remote_copy(
                src, dst, send_sem.at[t, FIRST[kind] + k], recv_sem.at[t, FIRST[kind] + k], device_id=device, device_id_type=MESH
            )
            for k, (src, dst, device) in enumerate(triples, first)
        ]

    def core_copies(b, t):
        return copies(CORE + b * BACK, t, [(ship.at[b, t, 1 - core], got_core.at[b, t], twin)])

    def y_copies(b, t):
        return copies(
            Y + b * BACK, t, [(ship_y.at[b, t, turn(y, d)], got_y.at[b, t, d - 1], along_y[d - 1]) for d in (1, 2, 3)]
        )

    def z_copies(b, t):
        return copies(Z + b * BACK, t, [(ship_z.at[b, t], got_z.at[b, t], far)])

    def share_y_copies(b, t):
        held = curv if b else act
        return copies(SHARE_Y + b * BACK, t, [(held.at[t, core, y], held.at[t, core, y], peer) for peer in along_y])

    def share_core_copy(b, t, d):
        piece = (curv if b else act).at[t, core, turn(y, 4 - d)]
        return copies(SHARE_CORE + b * BACK, t, [(piece, piece, twin)], d)[0]

    def share_core_copies(b, t):
        return [share_core_copy(b, t, d) for d in (0, 1, 2, 3)]

    def x_copies(t):
        return copies(X, t, [(ship_x.at[t, turn(x, d)], got_x.at[t, d - 1], along_x[d - 1]) for d in (1, 2, 3)])

    def l_copies(t):
        return copies(L, t, [(ship_l.at[t, turn(low, d)], got_l.at[t, d - 1], along_l[d - 1]) for d in (1, 2, 3)])

    def share_l_copies(t):
        return copies(SHARE_L, t, [(resid.at[t, x, low], resid.at[t, x, low], peer) for peer in along_l])

    def share_x_copies(t):
        return copies(SHARE_X, t, [(resid.at[t, x], resid.at[t, x], peer) for peer in along_x])

    def start(some):
        for copy in some[1:2] + some[:1] + some[2:]:
            copy.start()

    def arrived(some):
        for copy in some:
            copy.wait_recv()

    def sent(some):
        for copy in some:
            copy.wait_send()

    def add_arrivals(total, some, refs):
        for k in (0, 2, 1):
            some[k].wait_recv()
            total += wide(refs(k))
        return total

    def wide(ref):
        return ref[...].astype(F32)

    def flat(value):
        return value.astype(F32).reshape(-1, value.shape[-1]).astype(BF16)

    def put(b, t, which, partial):
        ship[b, t, :, :, which] = partial.reshape(2, 4, rows, ff).astype(BF16)

    def pre_partials(g):
        some = x_t[:, pl.ds(pl.multiple_of(g * GROUP, GROUP), GROUP)].T
        parts = pl.ds(g * per, per)
        ship[0, parts, :, :, 0] = dot(some, w_in_v[...]).reshape(per, 2, 4, rows, ff).astype(BF16)
        ship[0, parts, :, :, 1] = dot(some, p_in_v[...]).reshape(per, 2, 4, rows, ff).astype(BF16)

    def sum_cores(b, t):
        before = core_copies(b, t)
        arrived(before)
        ship_y[b, t] = (wide(ship.at[b, t, core]) + wide(got_core.at[b, t])).astype(BF16)
        start(y_copies(b, t))
        sent(before)

    def sum_y(b, t):
        before = y_copies(b, t)
        total = wide(ship.at[b, t, core, y]) + wide(got_core.at[b, t, y])
        total = add_arrivals(total, before, lambda k: got_y.at[b, t, k])
        ship_z[b, t] = total.astype(BF16)
        kept[b, t] = total
        start(z_copies(b, t))
        sent(before)

    def sum_z(b, t):
        arrived(z_copies(b, t))
        total = kept[b, t] + wide(got_z.at[b, t])
        return total[0], total[1]

    def activate(t):
        pre, pre_t = sum_z(0, t)
        pre_t = scale_in * pre_t
        value, slope, bend = gelu_parts(pre)
        act[t, core, y, 0] = value.astype(BF16)
        act[t, core, y, 1] = (slope * pre_t).astype(BF16)
        start(share_y_copies(0, t))
        share_core_copy(0, t, 0).start()
        sent(z_copies(0, t))
        slope_v[t] = slope
        bend_v[t] = bend * pre_t

    def pass_on(b, t):
        arrive = share_y_copies(b, t)
        for d in (1, 3, 2):
            arrive[d - 1].wait_recv()
            share_core_copy(b, t, d).start()
        sent(arrive)

    def out_partials(t):
        before = share_core_copies(0, t)
        arrived(before)
        some, some_t = flat(act[t, :, :, 0]), flat(act[t, :, :, 1])
        out = dot(some, w_out_v[...])
        out_t = dot(some_t, w_out_v[...]) + scale_out * dot(some, p_out_v[...])
        ship_x[t, 0:2] = out.reshape(2, 4, rows, width).astype(BF16)
        ship_x[t, 2:4] = out_t.reshape(2, 4, rows, width).astype(BF16)
        start(x_copies(t))
        sent(before)

    def sum_x(t):
        before = x_copies(t)
        total = add_arrivals(wide(ship_x.at[t, x]), before, lambda k: got_x.at[t, k])
        ship_l[t] = total.astype(BF16)
        start(l_copies(t))
        sent(before)

    def residuals(t):
        before = l_copies(t)
        total = wide(ship_x.at[t, x, low])
        for k in range(3):
            total += wide(got_x.at[t, k, low])
        total = add_arrivals(total, before, lambda k: got_l.at[t, k])
        first = t * part + lax.rem(x, 2) * (part // 2) + low * rows
        wanted = tgt_v[pl.ds(pl.multiple_of(first, rows), rows), :]
        wanted = wanted * (x < 2).astype(F32)
        resid[t, x, low] = (loss_scale * (total - wanted)).astype(BF16)
        start(share_l_copies(t))
        sent(before)

    def pass_on_x(t):
        before = share_l_copies(t)
        arrived(before)
        start(share_x_copies(t))
        sent(before)

    def back_partials(t):
        before = share_x_copies(t)
        arrived(before)
        some, some_t = flat(resid[t, 0:2]), flat(resid[t, 2:4])
        back = dot(some, w_out_t[...])
        back_t = dot(some_t, w_out_t[...]) + scale_out * dot(some, p_out_t[...])
        put(1, t, 0, back)
        put(1, t, 1, back_t)
        start(core_copies(1, t))
        sent(before)

    def curvature(t):
        back, back_t = sum_z(1, t)
        curv[t, core, y] = (back_t * slope_v[t] + back * bend_v[t]).astype(BF16)
        start(share_y_copies(1, t))
        share_core_copy(1, t, 0).start()
        sent(z_copies(1, t))

    def whole_curv(t):
        before = share_core_copies(1, t)
        arrived(before)
        sent(before)

    def turn_w():
        loads[3].wait()
        for i in range(ff // 128):
            w_out_v[i * 128 : (i + 1) * 128, :] = w_out_t[:, i * 128 : (i + 1) * 128].T

    def turn_p():
        loads[4].wait()
        for i in range(ff // 128):
            p_out_v[i * 128 : (i + 1) * 128, :] = p_out_t[:, i * 128 : (i + 1) * 128].T

    def turn_target():
        loads[5].wait()
        for i in range(tokens // 128):
            tgt_v[i * 128 : (i + 1) * 128, :] = tgt_t[:, i * 128 : (i + 1) * 128].T.astype(F32)

    def outer_out():
        resid_t[...] = flat(resid[:, 0:2]).T
        resid_tt[...] = flat(resid[:, 2:4]).T

        @pl.loop(0, ff // 384)
        def _(i):
            cols = pl.ds(pl.multiple_of(i * 384, 384), 384)
            some, some_t = flat(act[:, :, :, 0, :, cols]), flat(act[:, :, :, 1, :, cols])
            hess_out[:, cols] = (dot(resid_t[...], some_t) + dot(resid_tt[...], some)).astype(BF16)

    def outer_in(first, last, add):
        some = flat(curv[first:last])

        @pl.loop(0, width // 192)
        def _(i):
            cut = pl.ds(pl.multiple_of(i * 192, 192), 192)
            product = dot(x_t[cut, first * part : last * part], some)
            if add:
                hess_in[cut, :] = (outer[cut, :] + product).astype(BF16)
            else:
                outer[cut, :] = product

    def next_partials(t):
        if per == 1:
            pre_partials(t)
        else:
            pl.when(lax.rem(t, per) == 0)(lambda: pre_partials(t // per))

    steps = [
        (-1.5, next_partials),
        (0.0, lambda t: start(core_copies(0, t))),
        (5.3, lambda t: sum_cores(0, t)),
        (11.2, lambda t: sum_y(0, t)),
        (19.0, activate),
        (25.7, lambda t: pass_on(0, t)),
        (28.4, out_partials),
        (34.5, sum_x),
        (39.7, residuals),
        (45.3, pass_on_x),
        (52.2, back_partials),
        (54.0, lambda t: sum_cores(1, t)),
        (60.3, lambda t: sum_y(1, t)),
        (71.4, curvature),
        (78.0, lambda t: pass_on(1, t)),
        (83.3, whole_curv),
    ]
    order = sorted(((when % PERIOD, int(when // PERIOD), step) for when, step in steps), key=lambda entry: entry[0])
    last_tick = max(stage for _, stage, _ in order)
    back_tick = int(52.2 // PERIOD) + PARTS - 1

    for load in loads[:3]:
        load.wait()
    pre_partials(0)
    pl.semaphore_wait(barrier, len(peers))

    def tick(i, _):
        for _, stage, step in order:
            t = i - stage

            @pl.when((t >= max(0, -stage)) & (t < PARTS))
            def _(step=step, t=t):
                step(t)

        pl.when(i == 1)(turn_w)
        pl.when(i == 2)(turn_p)
        pl.when(i == 3)(turn_target)
        pl.when(i == back_tick)(outer_out)
        pl.when(i == last_tick + PARTS - per - 1)(lambda: outer_in(0, PARTS - per, False))
        return 0

    lax.fori_loop(0, last_tick + PARTS, tick, 0)

    outer_in(PARTS - per, PARTS, True)


def on_device(inputs, target, w_in, w_out, probe_in, probe_out):
    tokens, width = inputs.shape
    ff = w_in.shape[1]
    part = tokens // PARTS
    rows = part // 8
    n = PARTS
    hess_in, hess_out = pl.pallas_call(
        kernel,
        out_shape=(pltpu.VMEM((width, ff), BF16), pltpu.VMEM((width, ff), BF16)),
        in_specs=[pl.BlockSpec(memory_space=pl.ANY)] * 6,
        out_specs=(pl.BlockSpec(memory_space=pltpu.VMEM),) * 2,
        scratch_shapes=[
            pltpu.VMEM((width, tokens), BF16),
            pltpu.VMEM((width, tokens), BF16),
            pltpu.VMEM((tokens, width), F32),
            pltpu.VMEM((width, ff), BF16),
            pltpu.VMEM((width, ff), BF16),
            pltpu.VMEM((width, ff), BF16),
            pltpu.VMEM((width, ff), BF16),
            pltpu.VMEM((ff, width), BF16),
            pltpu.VMEM((ff, width), BF16),
            pltpu.VMEM((width, tokens), BF16),
            pltpu.VMEM((width, tokens), BF16),
            pltpu.VMEM((width, ff), F32),
            pltpu.VMEM((2, n, 2, 4, 2, rows, ff), BF16),
            pltpu.VMEM((2, n, 4, 2, rows, ff), BF16),
            pltpu.VMEM((2, n, 4, 2, rows, ff), BF16),
            pltpu.VMEM((2, n, 3, 2, rows, ff), BF16),
            pltpu.VMEM((2, n, 2, rows, ff), BF16),
            pltpu.VMEM((2, n, 2, rows, ff), BF16),
            pltpu.VMEM((2, n, 2, rows, ff), F32),
            pltpu.VMEM((n, 2, 4, 2, rows, ff), BF16),
            pltpu.VMEM((n, rows, ff), F32),
            pltpu.VMEM((n, rows, ff), F32),
            pltpu.VMEM((n, 2, 4, rows, ff), BF16),
            pltpu.VMEM((n, 4, 4, rows, width), BF16),
            pltpu.VMEM((n, 3, 4, rows, width), BF16),
            pltpu.VMEM((n, 4, rows, width), BF16),
            pltpu.VMEM((n, 3, rows, width), BF16),
            pltpu.VMEM((n, 4, 4, rows, width), BF16),
            pltpu.SemaphoreType.DMA((6,)),
            pltpu.SemaphoreType.DMA((n, SEMS)),
            pltpu.SemaphoreType.DMA((n, SEMS)),
        ],
        compiler_params=pltpu.CompilerParams(
            collective_id=0, has_side_effects=True, vmem_limit_bytes=56 * 1024 * 1024
        ),
        cost_estimate=pl.CostEstimate(
            flops=22 * tokens * width * ff, bytes_accessed=12 * width * ff, transcendentals=0
        ),
    )(inputs.T, target.T, w_in, w_out.T, probe_in, probe_out.T)
    return hess_in, hess_out.T


def solution(mesh):
    placed = (
        P(None, "row"),
        P(None, "row"),
        P("row", "col"),
        P("col", "row"),
        P("row", "col"),
        P("col", "row"),
    )
    return jax.shard_map(
        on_device,
        mesh=mesh,
        in_specs=placed,
        out_specs=(P("row", "col"), P("col", "row")),
        check_vma=False,
    )
```
